512 devices in a mesh: section: 16 (over x, z_hi), seq: 32 (over z_lo, y, core).
Axes of the slice: x: 4, y: 4, z: 16 (z_hi: 4, z_lo: 4; z = z_hi * 4 + z_lo), core: 2. Of those that a mesh axis runs over, the one named last changes fastest.
Arguments:
- section_states: bfloat16 [16, 2048, 4096], P('section', 'seq'), may hold values from -6 to 6
- dec_states: bfloat16 [16, 512, 4096], P('section', 'seq'), may hold values from -6 to 6
- norm_gain: float32 [16, 4096], P('section'), may hold values from 0.5 to 90
- w_query: bfloat16 [16, 4096, 4096], P('section', None, 'seq'), may hold values from -0.09375 to 0.09375
- w_key: bfloat16 [16, 4096, 4096], P('section', None, 'seq'), may hold values from -0.09375 to 0.09375
- w_value: bfloat16 [16, 4096, 4096], P('section', None, 'seq'), may hold values from -0.09375 to 0.09375
Outputs:
- context: bfloat16 [16, 512, 4096], P('section', 'seq')
The draws below stay inside these ranges and needn't reach their ends.
All inputs are finite; a program needn't handle non-finite values.
Results may differ from the reference program's by a relative error of at most 0.04.
The reference program's roundings to bfloat16 on the way count: a program that leaves them out, or rounds other values in their place, can miss the bound.
Values may be sent and summed in bfloat16 or wider, within the bound.
No kernel may reach another device: no remote copies, remote signals or barrier semaphores. Data moves between devices by JAX's collectives and lax.ppermute only.
A program may use at most 128 MiB of HBM per device.

```python
import jax
import jax.numpy as jnp
from jax import lax

D = 4096
HEADS = 16
HD = 256
ENC = 2048
DEC = 512
N_SECTION = 16


def draw_norm_gain(key, part):
    key = jax.random.fold_in(key, 11)
    values_drawn = jax.random.uniform(key, (N_SECTION, D), jnp.float32, 0.5, 1.5)
    return values_drawn


def shard_levels(rng, dims, cuts, least, high):
    factor_of, own = 1.0, jax.random.fold_in(rng, 6)
    for axis_at, parts in cuts:
        draws = jnp.exp(jax.random.uniform(jax.random.fold_in(own, axis_at), (parts,), jnp.float32, least / len(cuts), high / len(cuts)))
        factor_of = factor_of * jnp.repeat(draws, dims[axis_at] // parts).reshape([-1 if axis == axis_at else 1 for axis in range(len(dims))])
    return factor_of


def bell_draw(own_key, extent, width, most, split=(), held_as=jnp.bfloat16):
    array = jax.random.normal(own_key, extent, jnp.float32) * width
    if len(split) > 0:
        array = shard_levels(own_key, extent, split, -0.22, 0.18) * array
    return jnp.clip(array, min=-most, max=most).astype(held_as)


def setup_inputs(seed: int = 0) -> dict:
    arg_keys = jax.random.split(jax.random.key(seed), 7)
    section_states = bell_draw(arg_keys[0], (N_SECTION, ENC, D), 1.0, 6.0, ((0, 16), (1, 32)))
    dec_states = bell_draw(arg_keys[1], (N_SECTION, DEC, D), 1.0, 6.0, ((0, 16), (1, 32)))
    norm_gain = draw_norm_gain(jax.random.fold_in(arg_keys[6], 71), 0)
    w_query = bell_draw(arg_keys[3], (N_SECTION, D, D), D ** -0.5, 0.09375, ((0, 16), (2, 32)))
    w_key = bell_draw(arg_keys[4], (N_SECTION, D, D), D ** -0.5, 0.09375, ((0, 16), (2, 32)))
    w_value = bell_draw(arg_keys[5], (N_SECTION, D, D), D ** -0.5, 0.09375, ((0, 16), (2, 32)))
    return dict(section_states=section_states, dec_states=dec_states, norm_gain=norm_gain, w_query=w_query, w_key=w_key, w_value=w_value)


def section_layer(operands, final_rows):
    dec_rows, gain_row, query_weight, key_weight, value_weight = operands
    states = dec_rows.astype(jnp.float32)
    mean_square = lax.optimization_barrier(jnp.mean(states * states, axis=-1, keepdims=True))
    normed = (states * lax.rsqrt(mean_square + 1e-06) * gain_row).astype(jnp.bfloat16)
    queries = jnp.dot(normed, query_weight, preferred_element_type=jnp.float32).astype(jnp.bfloat16)
    keys_all = jnp.dot(final_rows, key_weight, preferred_element_type=jnp.float32).astype(jnp.bfloat16)
    values_all = jnp.dot(final_rows, value_weight, preferred_element_type=jnp.float32).astype(jnp.bfloat16)
    query_heads = queries.reshape(DEC, HEADS, HD).astype(jnp.float32)
    key_heads = keys_all.reshape(ENC, HEADS, HD).astype(jnp.float32)
    value_heads = values_all.reshape(ENC, HEADS, HD).astype(jnp.float32)
    scores = jnp.einsum('qhd,khd->hqk', query_heads, key_heads) * HD ** (-0.5)
    row_top = lax.optimization_barrier(jnp.max(scores, axis=-1, keepdims=True))
    weights_soft = jnp.exp(scores - row_top).astype(jnp.bfloat16)
    denom_sum = lax.optimization_barrier(jnp.sum(weights_soft.astype(jnp.float32), axis=-1))
    numer_sum = jnp.einsum('hqk,khd->qhd', weights_soft.astype(jnp.float32), value_heads)
    context = numer_sum / jnp.transpose(denom_sum)[:, :, None]
    return context.astype(jnp.bfloat16).reshape(DEC, D)

def reference(section_states, dec_states, norm_gain, w_query, w_key, w_value):
    final_rows = section_states[0]
    return lax.map(lambda operands: section_layer(operands, final_rows), (dec_states, norm_gain, w_query, w_key, w_value))
```

```python
import functools

import jax
import jax.numpy as jnp
import numpy as np
from jax import lax
from jax.experimental import pallas as pl
from jax.experimental.pallas import tpu as pltpu
from jax.sharding import Mesh, PartitionSpec as P

HD = 256
AXES = ("x", "zh", "zl", "y", "core")
SIZES = (4, 4, 4, 4, 2)
SECTION = ("x", "zh")
SEQ = ("zl", "y", "core")


def pairs_of(target):
    pairs = []
    for source in range(int(np.prod(SIZES))):
        place = target(*(int(v) for v in np.unravel_index(source, SIZES)))
        if place is not None:
            pairs.append((source, int(np.ravel_multi_index(place, SIZES))))
    return pairs


def shift(dx, dy, dz):
    def target(x, zh, zl, y, core):
        sign = -1 if core else 1
        z = (zh * 4 + zl + sign * dz) % 16
        return ((x + sign * dx) % 4, z // 4, z % 4, (y + sign * dy) % 4, core)

    return pairs_of(target)


def send(value, pairs):
    return lax.ppermute(value, AXES, pairs)


def scatter_x(block):
    x = lax.axis_index("x")
    rows = block.shape[0] // 4
    quarters = [block[i * rows : (i + 1) * rows] for i in range(4)]
    got = quarters[0]
    for i in (2, 1, 3):
        pairs = pairs_of(lambda cx, zh, zl, y, c: (i, zh, zl, y, c) if cx == 0 and zh == 0 else None)
        got = jnp.where(x == i, send(quarters[i], pairs), got)
    return got


def spread_z(piece):
    zh = lax.axis_index("zh")
    core = lax.axis_index("core")
    first = pairs_of(
        lambda x, h, zl, y, c: (x, 3 if c else 1, zl, y, c) if h == 0 else None
    )

    def second_target(x, h, zl, y, c):
        near, far = (3, 1) if c else (1, 3)
        if h == 0:
            return (x, far, zl, y, c)
        if h == near:
            return (x, 2, zl, y, c)
        return None

    near = jnp.where(core == 0, 1, 3)
    piece = jnp.where(zh == near, send(piece, first), piece)
    late = send(piece, pairs_of(second_target))
    return jnp.where((zh == 0) | (zh == near), piece, late)


def widen(block, moves):
    return [block] + [send(block, shift(*move)) for move in moves]


def attend_kernel(scale, query_ref, *refs):
    *kv_refs, own_ref, send_ref = refs
    query = query_ref[...]
    scores = []
    for kv in kv_refs:
        scores.append(
            lax.dot_general(
                query, kv[:, :HD], (((1,), (1,)), ((), ())), preferred_element_type=jnp.float32
            )
            * scale
        )
    top = functools.reduce(jnp.maximum, [jnp.max(s, axis=-1, keepdims=True) for s in scores])
    denom = jnp.zeros_like(top)
    numer = jnp.zeros((query.shape[0], HD), jnp.float32)
    for kv, s in zip(kv_refs, scores):
        probs = jnp.exp(s - top).astype(jnp.bfloat16)
        denom += jnp.sum(probs.astype(jnp.float32), axis=-1, keepdims=True)
        numer += jnp.dot(probs, kv[:, HD:], preferred_element_type=jnp.float32)
    half = HD // 2
    lane = lax.broadcasted_iota(jnp.int32, (query.shape[0], half), 1)
    stats = jnp.where(lane < half // 2, top, denom)
    own_ref[:, :half] = numer[:, :half]
    own_ref[:, half:] = stats
    send_ref[:, :half] = numer[:, half:]
    send_ref[:, half:] = stats


def attend(queries, key_values):
    count = queries.shape[0]
    block = 128
    out = jax.ShapeDtypeStruct((count, HD), jnp.float32)
    row_spec = pl.BlockSpec((block, HD), lambda i: (i, 0))
    keys = sum(kv.shape[0] for kv in key_values)
    return pl.pallas_call(
        functools.partial(attend_kernel, HD**-0.5),
        out_shape=(out, out),
        grid=(count // block,),
        in_specs=[row_spec] + [pl.BlockSpec(kv.shape, lambda i: (0, 0)) for kv in key_values],
        out_specs=(row_spec, row_spec),
        compiler_params=pltpu.CompilerParams(vmem_limit_bytes=40 * 2**20),
        cost_estimate=pl.CostEstimate(
            flops=4 * count * keys * HD,
            bytes_accessed=keys * HD * 4 + count * HD * 10,
            transcendentals=count * keys,
        ),
    )(queries, *key_values)


def local(section_states, dec_states, norm_gain, w_query, w_key, w_value):
    model_width = dec_states.shape[2]
    dec_count = dec_states.shape[1]
    seq_count = lax.axis_size(SEQ)
    half = HD // 2

    states = dec_states[0].astype(jnp.float32)
    mean_square = jnp.mean(states * states, axis=-1, keepdims=True)
    normed = (states * lax.rsqrt(mean_square + 1e-06) * norm_gain[0]).astype(jnp.bfloat16)
    normed_all = lax.all_gather(normed, SEQ, axis=0, tiled=True)

    other_core = pairs_of(lambda x, zh, zl, y, c: (x, zh, zl, y, 1 - c))
    mine = (w_key[0], w_value[0], w_query[0])
    other = [send(w, other_core) for w in mine]

    piece = spread_z(scatter_x(section_states[0]))
    piece = jnp.concatenate(widen(piece, ((2, 2, 2), (1, 1, -1), (-1, -1, 1))), axis=0)
    quarter = jnp.concatenate(widen(piece, ((1, 0, 1), (-1, 0, -1), (0, 2, 0))), axis=0)
    one_hop = ((1, 0, 0), (0, 1, 0), (0, 0, 1))
    middle = quarter.shape[0] // 2
    first = widen(quarter[:middle], one_hop)
    second = widen(quarter[middle:], one_hop)
    blocks = [quarter] + first[1:] + second[1:]

    kv_cols = jnp.concatenate([mine[0], other[0], mine[1], other[1]], axis=1)
    query_cols = jnp.concatenate([mine[2], other[2]], axis=1)
    queries = jnp.dot(normed_all, query_cols, preferred_element_type=jnp.float32).astype(jnp.bfloat16)
    key_values = [
        jnp.dot(rows, kv_cols, preferred_element_type=jnp.float32).astype(jnp.bfloat16) for rows in blocks
    ]

    own, outgoing = attend(queries, key_values)
    arrived = send(outgoing, other_core)
    stat = lambda a: (a[:, half : half + 1], a[:, half + half // 2 : half + half // 2 + 1])
    (top_a, denom_a), (top_b, denom_b) = stat(own), stat(arrived)
    joint = jnp.maximum(top_a, top_b)
    factor_a, factor_b = jnp.exp(top_a - joint), jnp.exp(top_b - joint)
    numer = own[:, :half] * factor_a + arrived[:, :half] * factor_b
    merged = (numer / (denom_a * factor_a + denom_b * factor_b)).astype(jnp.bfloat16)

    parts = merged.reshape(seq_count, dec_count, half)
    returned = lax.all_to_all(parts, SEQ, split_axis=0, concat_axis=0, tiled=True)
    return jnp.transpose(returned, (1, 0, 2)).reshape(1, dec_count, model_width)


def solution(mesh):
    fine = Mesh(mesh.devices.reshape(SIZES), AXES)
    in_specs = (
        P(SECTION, SEQ, None),
        P(SECTION, SEQ, None),
        P(SECTION, None),
        P(SECTION, None, SEQ),
        P(SECTION, None, SEQ),
        P(SECTION, None, SEQ),
    )
    return jax.shard_map(
        local, mesh=fine, in_specs=in_specs, out_specs=P(SECTION, SEQ, None), check_vma=False
    )
```

```python
import functools

import jax
import jax.numpy as jnp
import numpy as np
from jax import lax
from jax.experimental import pallas as pl
from jax.experimental.pallas import tpu as pltpu
from jax.sharding import Mesh, PartitionSpec as P

HD = 256
AXES = ("x", "zh", "zl", "y", "core")
SIZES = (4, 4, 4, 4, 2)
SECTION = ("x", "zh")
SEQ = ("zl", "y", "core")


def pairs_of(target):
    pairs = []
    for source in range(int(np.prod(SIZES))):
        place = target(*(int(v) for v in np.unravel_index(source, SIZES)))
        if place is not None:
            pairs.append((source, int(np.ravel_multi_index(place, SIZES))))
    return pairs


def shift(dx, dy, dz):
    def target(x, zh, zl, y, core):
        sign = -1 if core else 1
        z = (zh * 4 + zl + sign * dz) % 16
        return ((x + sign * dx) % 4, z // 4, z % 4, (y + sign * dy) % 4, core)

    return pairs_of(target)


def send(value, pairs):
    return lax.ppermute(value, AXES, pairs)


def scatter_x(block):
    x = lax.axis_index("x")
    rows = block.shape[0] // 4
    quarters = [block[i * rows : (i + 1) * rows] for i in range(4)]
    got = quarters[0]
    for i in (2, 1, 3):
        pairs = pairs_of(lambda cx, zh, zl, y, c: (i, zh, zl, y, c) if cx == 0 and zh == 0 else None)
        got = jnp.where(x == i, send(quarters[i], pairs), got)
    return got


def spread_z(piece):
    zh = lax.axis_index("zh")
    core = lax.axis_index("core")
    first = pairs_of(
        lambda x, h, zl, y, c: (x, 3 if c else 1, zl, y, c) if h == 0 else None
    )

    def second_target(x, h, zl, y, c):
        near, far = (3, 1) if c else (1, 3)
        if h == 0:
            return (x, far, zl, y, c)
        if h == near:
            return (x, 2, zl, y, c)
        return None

    near = jnp.where(core == 0, 1, 3)
    piece = jnp.where(zh == near, send(piece, first), piece)
    late = send(piece, pairs_of(second_target))
    return jnp.where((zh == 0) | (zh == near), piece, late)


def widen(block, moves):
    return [block] + [send(block, shift(*move)) for move in moves]


def norm_kernel(states_ref, gain_ref, out_ref):
    states = states_ref[...].astype(jnp.float32)
    mean_square = jnp.mean(states * states, axis=-1, keepdims=True)
    out_ref[...] = (states * lax.rsqrt(mean_square + 1e-06) * gain_ref[...]).astype(jnp.bfloat16)


def attend_kernel(scale, query_ref, *refs):
    *kv_refs, own_ref, send_ref = refs
    query = query_ref[...]
    half = HD // 2
    keys = lambda kv: jnp.concatenate([kv[:, :half], kv[:, HD : HD + half]], axis=1)
    values = lambda kv: jnp.concatenate([kv[:, half:HD], kv[:, HD + half :]], axis=1)
    scores = []
    for kv in kv_refs:
        scores.append(
            lax.dot_general(
                query, keys(kv), (((1,), (1,)), ((), ())), preferred_element_type=jnp.float32
            )
            * scale
        )
    top = functools.reduce(jnp.maximum, [jnp.max(s, axis=-1, keepdims=True) for s in scores])
    denom = jnp.zeros_like(top)
    numer = jnp.zeros((query.shape[0], HD), jnp.float32)
    for kv, s in zip(kv_refs, scores):
        probs = jnp.exp(s - top).astype(jnp.bfloat16)
        denom += jnp.sum(probs.astype(jnp.float32), axis=-1, keepdims=True)
        numer += jnp.dot(probs, values(kv), preferred_element_type=jnp.float32)
    lane = lax.broadcasted_iota(jnp.int32, (query.shape[0], half), 1)
    stats = jnp.where(lane < half // 2, top, denom)
    own_ref[:, :half] = numer[:, :half]
    own_ref[:, half:] = stats
    send_ref[:, :half] = numer[:, half:]
    send_ref[:, half:] = stats


def attend(queries, key_values):
    count = queries.shape[0]
    block = 128
    out = jax.ShapeDtypeStruct((count, HD), jnp.float32)
    row_spec = pl.BlockSpec((block, HD), lambda i: (i, 0))
    keys = sum(kv.shape[0] for kv in key_values)
    return pl.pallas_call(
        functools.partial(attend_kernel, HD**-0.5),
        out_shape=(out, out),
        grid=(count // block,),
        in_specs=[row_spec] + [pl.BlockSpec(kv.shape, lambda i: (0, 0)) for kv in key_values],
        out_specs=(row_spec, row_spec),
        compiler_params=pltpu.CompilerParams(vmem_limit_bytes=40 * 2**20),
        cost_estimate=pl.CostEstimate(
            flops=4 * count * keys * HD,
            bytes_accessed=keys * HD * 4 + count * HD * 10,
            transcendentals=count * keys,
        ),
    )(queries, *key_values)


def local(section_states, dec_states, norm_gain, w_query, w_key, w_value):
    model_width = dec_states.shape[2]
    dec_count = dec_states.shape[1]
    seq_count = lax.axis_size(SEQ)
    half = HD // 2

    normed = pl.pallas_call(
        norm_kernel, out_shape=jax.ShapeDtypeStruct(dec_states.shape[1:], jnp.bfloat16)
    )(dec_states[0], norm_gain)
    encoder_rows, normed = lax.optimization_barrier((section_states[0], normed))
    normed_all = lax.all_gather(normed, SEQ, axis=0, tiled=True)

    piece = scatter_x(encoder_rows)

    other_core = pairs_of(lambda x, zh, zl, y, c: (x, zh, zl, y, 1 - c))
    kv_mine = jnp.concatenate([w_key[0], w_value[0]], axis=1)
    piece, kv_mine, query_mine = lax.optimization_barrier((piece, kv_mine, w_query[0]))
    kv_other, query_other = send(kv_mine, other_core), send(query_mine, other_core)
    piece = spread_z(piece)
    piece, kv_other, query_other = lax.optimization_barrier((piece, kv_other, query_other))

    piece = jnp.concatenate(widen(piece, ((2, 2, 2), (1, 1, -1), (-1, -1, 1))), axis=0)
    quarter = jnp.concatenate(widen(piece, ((1, 0, 1), (-1, 0, -1), (0, 2, 0))), axis=0)
    _, *arrived = widen(quarter, ((1, 0, 0), (0, 1, 0), (0, 0, 1)))

    kv_cols = jnp.concatenate([kv_mine, kv_other], axis=1)
    query_cols = jnp.concatenate([query_mine, query_other], axis=1)
    queries = jnp.dot(normed_all, query_cols, preferred_element_type=jnp.float32).astype(jnp.bfloat16)
    project = lambda rows: jnp.dot(rows, kv_cols, preferred_element_type=jnp.float32).astype(jnp.bfloat16)
    near = project(quarter)
    queries, near, *arrived = lax.optimization_barrier((queries, near, *arrived))
    key_values = [near] + [project(rows) for rows in arrived]

    own, outgoing = attend(queries, key_values)
    arrived = send(outgoing, other_core)
    stat = lambda a: (a[:, half : half + 1], a[:, half + half // 2 : half + half // 2 + 1])
    (top_a, denom_a), (top_b, denom_b) = stat(own), stat(arrived)
    joint = jnp.maximum(top_a, top_b)
    factor_a, factor_b = jnp.exp(top_a - joint), jnp.exp(top_b - joint)
    numer = own[:, :half] * factor_a + arrived[:, :half] * factor_b
    merged = (numer / (denom_a * factor_a + denom_b * factor_b)).astype(jnp.bfloat16)

    parts = merged.reshape(seq_count, dec_count, half)
    returned = lax.all_to_all(parts, SEQ, split_axis=0, concat_axis=0, tiled=True)
    return jnp.transpose(returned, (1, 0, 2)).reshape(1, dec_count, model_width)


def solution(mesh):
    fine = Mesh(mesh.devices.reshape(SIZES), AXES)
    in_specs = (
        P(SECTION, SEQ, None),
        P(SECTION, SEQ, None),
        P(SECTION, None),
        P(SECTION, None, SEQ),
        P(SECTION, None, SEQ),
        P(SECTION, None, SEQ),
    )
    return jax.shard_map(
        local, mesh=fine, in_specs=in_specs, out_specs=P(SECTION, SEQ, None), check_vma=False
    )
```

```python
import functools

import jax
import jax.numpy as jnp
import numpy as np
from jax import lax
from jax.experimental import pallas as pl
from jax.experimental.pallas import tpu as pltpu
from jax.sharding import Mesh, PartitionSpec as P

HD = 256
AXES = ("x", "zh", "zl", "y", "core")
SIZES = (4, 4, 4, 4, 2)
SECTION = ("x", "zh")
SEQ = ("zl", "y", "core")


def pairs_of(target):
    pairs = []
    for source in range(int(np.prod(SIZES))):
        place = target(*(int(v) for v in np.unravel_index(source, SIZES)))
        if place is not None:
            pairs.append((source, int(np.ravel_multi_index(place, SIZES))))
    return pairs


def shift(dx, dy, dz):
    def target(x, zh, zl, y, core):
        sign = -1 if core else 1
        z = (zh * 4 + zl + sign * dz) % 16
        return ((x + sign * dx) % 4, z // 4, z % 4, (y + sign * dy) % 4, core)

    return pairs_of(target)


def send(value, pairs):
    return lax.ppermute(value, AXES, pairs)


def scatter_x(block):
    x = lax.axis_index("x")
    rows = block.shape[0] // 4
    quarters = [block[i * rows : (i + 1) * rows] for i in range(4)]
    got = quarters[0]
    for i in (2, 1, 3):
        pairs = pairs_of(lambda cx, zh, zl, y, c: (i, zh, zl, y, c) if cx == 0 and zh == 0 else None)
        got = jnp.where(x == i, send(quarters[i], pairs), got)
    return got


def spread_z(piece):
    zh = lax.axis_index("zh")
    core = lax.axis_index("core")
    first = pairs_of(
        lambda x, h, zl, y, c: (x, 3 if c else 1, zl, y, c) if h == 0 else None
    )

    def second_target(x, h, zl, y, c):
        near, far = (3, 1) if c else (1, 3)
        if h == 0:
            return (x, far, zl, y, c)
        if h == near:
            return (x, 2, zl, y, c)
        return None

    near = jnp.where(core == 0, 1, 3)
    piece = jnp.where(zh == near, send(piece, first), piece)
    late = send(piece, pairs_of(second_target))
    return jnp.where((zh == 0) | (zh == near), piece, late)


def widen(block, moves):
    return [block] + [send(block, shift(*move)) for move in moves]


def norm_kernel(states_ref, gain_ref, out_ref):
    states = states_ref[...].astype(jnp.float32)
    mean_square = jnp.mean(states * states, axis=-1, keepdims=True)
    out_ref[...] = (states * lax.rsqrt(mean_square + 1e-06) * gain_ref[...]).astype(jnp.bfloat16)


def attend_kernel(scale, query_ref, *refs):
    *kv_refs, own_ref, send_ref = refs
    query = query_ref[...]
    half = HD // 2
    keys = lambda kv: jnp.concatenate([kv[:, :half], kv[:, HD : HD + half]], axis=1)
    values = lambda kv: jnp.concatenate([kv[:, half:HD], kv[:, HD + half :]], axis=1)
    scores = []
    for kv in kv_refs:
        scores.append(
            lax.dot_general(
                query, keys(kv), (((1,), (1,)), ((), ())), preferred_element_type=jnp.float32
            )
            * scale
        )
    top = functools.reduce(jnp.maximum, [jnp.max(s, axis=-1, keepdims=True) for s in scores])
    denom = jnp.zeros_like(top)
    numer = jnp.zeros((query.shape[0], HD), jnp.float32)
    for kv, s in zip(kv_refs, scores):
        probs = jnp.exp(s - top).astype(jnp.bfloat16)
        denom += jnp.sum(probs.astype(jnp.float32), axis=-1, keepdims=True)
        numer += jnp.dot(probs, values(kv), preferred_element_type=jnp.float32)
    lane = lax.broadcasted_iota(jnp.int32, (query.shape[0], half), 1)
    stats = jnp.where(lane < half // 2, top, denom)
    own_ref[:, :half] = numer[:, :half]
    own_ref[:, half:] = stats
    send_ref[:, :half] = numer[:, half:]
    send_ref[:, half:] = stats


def attend(queries, key_values):
    count = queries.shape[0]
    block = 128
    out = jax.ShapeDtypeStruct((count, HD), jnp.float32)
    row_spec = pl.BlockSpec((block, HD), lambda i: (i, 0))
    keys = sum(kv.shape[0] for kv in key_values)
    return pl.pallas_call(
        functools.partial(attend_kernel, HD**-0.5),
        out_shape=(out, out),
        grid=(count // block,),
        in_specs=[row_spec] + [pl.BlockSpec(kv.shape, lambda i: (0, 0)) for kv in key_values],
        out_specs=(row_spec, row_spec),
        compiler_params=pltpu.CompilerParams(vmem_limit_bytes=16 * 2**20),
        cost_estimate=pl.CostEstimate(
            flops=4 * count * keys * HD,
            bytes_accessed=keys * HD * 4 + count * HD * 10,
            transcendentals=count * keys,
        ),
    )(queries, *key_values)


def local(section_states, dec_states, norm_gain, w_query, w_key, w_value):
    model_width = dec_states.shape[2]
    dec_count = dec_states.shape[1]
    seq_count = lax.axis_size(SEQ)
    half = HD // 2

    normed = pl.pallas_call(
        norm_kernel,
        out_shape=jax.ShapeDtypeStruct(dec_states.shape[1:], jnp.bfloat16),
        compiler_params=pltpu.CompilerParams(vmem_limit_bytes=4 * 2**20),
    )(dec_states[0], norm_gain)
    encoder_rows, normed = lax.optimization_barrier((section_states[0], normed))
    normed_all = lax.all_gather(normed, SEQ, axis=0, tiled=True)

    piece = scatter_x(encoder_rows)

    other_core = pairs_of(lambda x, zh, zl, y, c: (x, zh, zl, y, 1 - c))
    kv_mine = jnp.concatenate([w_key[0], w_value[0]], axis=1)
    query_mine = w_query[0]
    kv_other, query_other = send(kv_mine, other_core), send(query_mine, other_core)
    piece = spread_z(piece)

    piece = jnp.concatenate(widen(piece, ((2, 2, 2), (1, 1, -1), (-1, -1, 1))), axis=0)
    _, a, b, c = widen(piece, ((1, 0, 1), (-1, 0, -1), (0, 2, 0)))
    one_hop = ((1, 0, 0), (0, 1, 0), (0, 0, 1))
    near_first, *first = widen(jnp.concatenate([piece, a], axis=0), one_hop)
    near_second, *second = widen(jnp.concatenate([b, c], axis=0), one_hop)

    kv_cols = jnp.concatenate([kv_mine, kv_other], axis=1)
    query_cols = jnp.concatenate([query_mine, query_other], axis=1)
    queries = jnp.dot(normed_all, query_cols, preferred_element_type=jnp.float32).astype(jnp.bfloat16)
    project = lambda rows: jnp.dot(rows, kv_cols, preferred_element_type=jnp.float32).astype(jnp.bfloat16)
    blocks = [near_first, near_second] + first
    for rows in second:
        blocks.append(lax.optimization_barrier((rows, queries))[0])
    key_values = [project(rows) for rows in blocks]

    own, outgoing = attend(queries, key_values)
    arrived = send(outgoing, other_core)
    stat = lambda a: (a[:, half : half + 1], a[:, half + half // 2 : half + half // 2 + 1])
    (top_a, denom_a), (top_b, denom_b) = stat(own), stat(arrived)
    joint = jnp.maximum(top_a, top_b)
    factor_a, factor_b = jnp.exp(top_a - joint), jnp.exp(top_b - joint)
    numer = own[:, :half] * factor_a + arrived[:, :half] * factor_b
    merged = (numer / (denom_a * factor_a + denom_b * factor_b)).astype(jnp.bfloat16)

    parts = merged.reshape(seq_count, dec_count, half)
    returned = lax.all_to_all(parts, SEQ, split_axis=0, concat_axis=0, tiled=True)
    return jnp.transpose(returned, (1, 0, 2)).reshape(1, dec_count, model_width)


def solution(mesh):
    fine = Mesh(mesh.devices.reshape(SIZES), AXES)
    in_specs = (
        P(SECTION, SEQ, None),
        P(SECTION, SEQ, None),
        P(SECTION, None),
        P(SECTION, None, SEQ),
        P(SECTION, None, SEQ),
        P(SECTION, None, SEQ),
    )
    return jax.shard_map(
        local, mesh=fine, in_specs=in_specs, out_specs=P(SECTION, SEQ, None), check_vma=False
    )
```

```python
import functools

import jax
import jax.numpy as jnp
import numpy as np
from jax import lax
from jax.experimental import pallas as pl
from jax.experimental.pallas import tpu as pltpu
from jax.sharding import Mesh, PartitionSpec as P

HD = 256
AXES = ("x", "zh", "zl", "y", "core")
SIZES = (4, 4, 4, 4, 2)
SECTION = ("x", "zh")
SEQ = ("zl", "y", "core")


def pairs_of(target):
    pairs = []
    for source in range(int(np.prod(SIZES))):
        place = target(*(int(v) for v in np.unravel_index(source, SIZES)))
        if place is not None:
            pairs.append((source, int(np.ravel_multi_index(place, SIZES))))
    return pairs


def shift(dx, dy, dz):
    def target(x, zh, zl, y, core):
        sign = -1 if core else 1
        z = (zh * 4 + zl + sign * dz) % 16
        return ((x + sign * dx) % 4, z // 4, z % 4, (y + sign * dy) % 4, core)

    return pairs_of(target)


def send(value, pairs):
    return lax.ppermute(value, AXES, pairs)


def scatter_x(block):
    x = lax.axis_index("x")
    rows = block.shape[0] // 4
    quarters = [block[i * rows : (i + 1) * rows] for i in range(4)]
    got = quarters[0]
    for i in (2, 1, 3):
        pairs = pairs_of(lambda cx, zh, zl, y, c: (i, zh, zl, y, c) if cx == 0 and zh == 0 else None)
        got = jnp.where(x == i, send(quarters[i], pairs), got)
    return got


def spread_z(piece):
    zh = lax.axis_index("zh")
    core = lax.axis_index("core")
    first = pairs_of(
        lambda x, h, zl, y, c: (x, 3 if c else 1, zl, y, c) if h == 0 else None
    )

    def second_target(x, h, zl, y, c):
        near, far = (3, 1) if c else (1, 3)
        if h == 0:
            return (x, far, zl, y, c)
        if h == near:
            return (x, 2, zl, y, c)
        return None

    near = jnp.where(core == 0, 1, 3)
    piece = jnp.where(zh == near, send(piece, first), piece)
    late = send(piece, pairs_of(second_target))
    return jnp.where((zh == 0) | (zh == near), piece, late)


def widen(block, moves):
    return [block] + [send(block, shift(*move)) for move in moves]


def norm_kernel(states_ref, gain_ref, out_ref):
    states = states_ref[...].astype(jnp.float32)
    mean_square = jnp.mean(states * states, axis=-1, keepdims=True)
    out_ref[...] = (states * lax.rsqrt(mean_square + 1e-06) * gain_ref[...]).astype(jnp.bfloat16)


def attend_kernel(scale, query_ref, *refs):
    *kv_refs, own_ref, send_ref = refs
    query = query_ref[...]
    half = HD // 2
    keys = lambda kv: jnp.concatenate([kv[:, :half], kv[:, HD : HD + half]], axis=1)
    values = lambda kv: jnp.concatenate([kv[:, half:HD], kv[:, HD + half :]], axis=1)
    scores = []
    for kv in kv_refs:
        scores.append(
            lax.dot_general(
                query, keys(kv), (((1,), (1,)), ((), ())), preferred_element_type=jnp.float32
            )
            * scale
        )
    top = functools.reduce(jnp.maximum, [jnp.max(s, axis=-1, keepdims=True) for s in scores])
    denom = jnp.zeros_like(top)
    numer = jnp.zeros((query.shape[0], HD), jnp.float32)
    for kv, s in zip(kv_refs, scores):
        probs = jnp.exp(s - top).astype(jnp.bfloat16)
        denom += jnp.sum(probs.astype(jnp.float32), axis=-1, keepdims=True)
        numer += jnp.dot(probs, values(kv), preferred_element_type=jnp.float32)
    lane = lax.broadcasted_iota(jnp.int32, (query.shape[0], half), 1)
    stats = jnp.where(lane < half // 2, top, denom)
    own_ref[:, :half] = numer[:, :half]
    own_ref[:, half:] = stats
    send_ref[:, :half] = numer[:, half:]
    send_ref[:, half:] = stats


def attend(queries, key_values):
    count = queries.shape[0]
    block = 128
    out = jax.ShapeDtypeStruct((count, HD), jnp.float32)
    row_spec = pl.BlockSpec((block, HD), lambda i: (i, 0))
    keys = sum(kv.shape[0] for kv in key_values)
    return pl.pallas_call(
        functools.partial(attend_kernel, HD**-0.5),
        out_shape=(out, out),
        grid=(count // block,),
        in_specs=[row_spec] + [pl.BlockSpec(kv.shape, lambda i: (0, 0)) for kv in key_values],
        out_specs=(row_spec, row_spec),
        compiler_params=pltpu.CompilerParams(vmem_limit_bytes=16 * 2**20),
        cost_estimate=pl.CostEstimate(
            flops=4 * count * keys * HD,
            bytes_accessed=keys * HD * 4 + count * HD * 10,
            transcendentals=count * keys,
        ),
    )(queries, *key_values)


def local(section_states, dec_states, norm_gain, w_query, w_key, w_value):
    model_width = dec_states.shape[2]
    dec_count = dec_states.shape[1]
    seq_count = lax.axis_size(SEQ)
    half = HD // 2

    normed = pl.pallas_call(
        norm_kernel,
        out_shape=jax.ShapeDtypeStruct(dec_states.shape[1:], jnp.bfloat16),
        compiler_params=pltpu.CompilerParams(vmem_limit_bytes=4 * 2**20),
    )(dec_states[0], norm_gain)
    encoder_rows, normed = lax.optimization_barrier((section_states[0], normed))
    normed_all = lax.all_gather(normed, SEQ, axis=0, tiled=True)

    piece = scatter_x(encoder_rows)

    other_core = pairs_of(lambda x, zh, zl, y, c: (x, zh, zl, y, 1 - c))
    kv_mine = jnp.concatenate([w_key[0], w_value[0]], axis=1)
    query_mine = w_query[0]
    kv_other, query_other = send(kv_mine, other_core), send(query_mine, other_core)
    piece = spread_z(piece)

    piece = jnp.concatenate(widen(piece, ((2, 2, 2),)), axis=0)
    piece = jnp.concatenate(widen(piece, ((1, 1, -1),)), axis=0)
    quarter = jnp.concatenate(widen(piece, ((1, 0, 1), (-1, 0, -1), (0, 2, 0))), axis=0)
    _, *arrived = widen(quarter, ((1, 0, 0), (0, 1, 0), (0, 0, 1)))

    kv_cols = jnp.concatenate([kv_mine, kv_other], axis=1)
    query_cols = jnp.concatenate([query_mine, query_other], axis=1)
    queries = jnp.dot(normed_all, query_cols, preferred_element_type=jnp.float32).astype(jnp.bfloat16)
    project = lambda rows: jnp.dot(rows, kv_cols, preferred_element_type=jnp.float32).astype(jnp.bfloat16)
    near = project(quarter)
    queries, near, arrived[0] = lax.optimization_barrier((queries, near, arrived[0]))
    key_values = [near] + [project(rows) for rows in arrived]

    own, outgoing = attend(queries, key_values)
    arrived = send(outgoing, other_core)
    stat = lambda a: (a[:, half : half + 1], a[:, half + half // 2 : half + half // 2 + 1])
    (top_a, denom_a), (top_b, denom_b) = stat(own), stat(arrived)
    joint = jnp.maximum(top_a, top_b)
    factor_a, factor_b = jnp.exp(top_a - joint), jnp.exp(top_b - joint)
    numer = own[:, :half] * factor_a + arrived[:, :half] * factor_b
    merged = (numer / (denom_a * factor_a + denom_b * factor_b)).astype(jnp.bfloat16)

    parts = merged.reshape(seq_count, dec_count, half)
    returned = lax.all_to_all(parts, SEQ, split_axis=0, concat_axis=0, tiled=True)
    return jnp.transpose(returned, (1, 0, 2)).reshape(1, dec_count, model_width)


def solution(mesh):
    fine = Mesh(mesh.devices.reshape(SIZES), AXES)
    in_specs = (
        P(SECTION, SEQ, None),
        P(SECTION, SEQ, None),
        P(SECTION, None),
        P(SECTION, None, SEQ),
        P(SECTION, None, SEQ),
        P(SECTION, None, SEQ),
    )
    return jax.shard_map(
        local, mesh=fine, in_specs=in_specs, out_specs=P(SECTION, SEQ, None), check_vma=False
    )
```
